512 devices in a mesh: section: 64 (over z_lo, x, y), tp: 8 (over z_hi, core).
Axes of the slice: x: 4, y: 8, z: 8 (z_hi: 4, z_lo: 2; z = z_hi * 2 + z_lo), core: 2. Of those that a mesh axis runs over, the one named last changes fastest.
Arguments:
- ctx_keys: bfloat16 [64, 6144, 1024], P('section', None, 'tp'), may hold values from -6 to 6
- ctx_values: bfloat16 [64, 6144, 1024], P('section', None, 'tp'), may hold values from -6 to 6
- span_q: bfloat16 [64, 64, 8192], P('section', None, 'tp'), may hold values from -140 to 140
- span_k: bfloat16 [64, 64, 1024], P('section', None, 'tp'), may hold values from -6 to 6
- span_v: bfloat16 [64, 64, 1024], P('section', None, 'tp'), may hold values from -6 to 6
- lengths: int32 [64], P('section'), may hold values from 768 to 6144, as said below
- group_lists: int32 [64, 4], replicated, may hold values from 0 to 63, as said below
- dec_q: bfloat16 [256, 2, 8192], P('section', None, 'tp'), may hold values from -140 to 140
- dec_k: bfloat16 [256, 2, 1024], P('section', None, 'tp'), may hold values from -6 to 6
- dec_v: bfloat16 [256, 2, 1024], P('section', None, 'tp'), may hold values from -6 to 6
- out_weight: bfloat16 [8192, 8192], P('tp', 'section'), may hold values from -0.0625 to 0.0625
Outputs:
- span_out: bfloat16 [64, 64, 8192], P('section', None, 'tp')
- dec_proj: bfloat16 [256, 2, 8192], P('tp', None, 'section')
The draws below stay inside these ranges and needn't reach their ends.
Inputs may be any that keep to these rules, and one draw needn't show every extreme that they name: `group_lists`: each row names 4 distinct groups, and every group is named by exactly 4 prompts, each in a different column. `lengths`: some prompt has exactly 6144.
All inputs are finite; a program needn't handle non-finite values.
Results may differ from the reference program's by a relative error of at most 0.0057.
Values may be sent and summed in bfloat16 or wider, within the bound.
A program may use at most 64 MiB of HBM per device.

```python
import jax
import jax.numpy as jnp
from jax import lax

D = 8192
QH = 64
KVH = 8
HD = 128
CTX = 6144
SPAN = 64
STEPS = 2
CAND_DEV = 4
PROMPTS = 64
CANDS = 256


def shared_keys(key):
    return jax.random.truncated_normal(key, -6.0, 6.0, (PROMPTS, CTX, KVH * HD), jnp.float32)


def shared_new_keys(key):
    return jax.random.truncated_normal(jax.random.fold_in(key, 21), -6.0, 6.0, (CANDS, STEPS, KVH * HD), jnp.float32)


def group_table(key):
    shuffle = jax.random.permutation(jax.random.fold_in(key, 4), PROMPTS).astype(jnp.int32)
    offsets = jnp.arange(CAND_DEV, dtype=jnp.int32)
    return ((shuffle[:, None] + offsets[None, :]) % PROMPTS).astype(jnp.int32)


def draw_ctx_keys(key, part):
    base = shared_keys(key)
    return base.astype(jnp.bfloat16)


def draw_span_q(key, part):
    key = jax.random.fold_in(key, 2)
    query = jax.random.truncated_normal(key, -6.0, 6.0, (PROMPTS, SPAN, QH * HD), jnp.float32)
    return query.astype(jnp.bfloat16)


def draw_lengths(key, part):
    key = jax.random.fold_in(key, 3)
    first, second = jax.random.split(key)
    values = jax.random.randint(first, (PROMPTS,), CTX // 8, CTX + 1, jnp.int32)
    order = jax.random.permutation(second, PROMPTS)
    return values.at[order[0]].set(CTX).astype(jnp.int32)


def draw_group_lists(key, part):
    return group_table(key)


def draw_dec_q(key, part):
    key = jax.random.fold_in(key, 6)
    query = jax.random.truncated_normal(key, -6.0, 6.0, (CANDS, STEPS, QH * HD), jnp.float32)
    return query.astype(jnp.bfloat16)


def draw_dec_k(key, part):
    base = shared_new_keys(key)
    return base.astype(jnp.bfloat16)


def block_scale(key, extent, cuts, low, high):
    def one(dim, shards_of):
        draws = jax.random.uniform(jax.random.fold_in(jax.random.fold_in(key, 6), dim), (shards_of,), jnp.float32, low / len(cuts), high / len(cuts))
        return jnp.repeat(jnp.exp(draws), extent[dim] // shards_of).reshape((-1,) + (1,) * (len(extent) - dim - 1))

    level = one(*cuts[0])
    for cut in cuts[1:]:
        level = level * one(*cut)
    return level


def normal_values(stream_key, shape, spread, most, cuts=(), kind=jnp.bfloat16):
    level = block_scale(stream_key, shape, cuts, -0.22, 0.18) if cuts else 1.0
    values = jax.random.normal(stream_key, shape, jnp.float32) * spread * level
    return jnp.minimum(jnp.maximum(values, -most), most).astype(kind)


def setup_inputs(seed: int = 0) -> dict:
    streams_of = jax.random.split(jax.random.key(seed), 12)
    ctx_keys = draw_ctx_keys(jax.random.fold_in(streams_of[11], 71), 0)
    ctx_values = normal_values(streams_of[1], (PROMPTS, CTX, KVH * HD), 1.0, 6.0, ((0, 64), (2, 8)))
    span_q = draw_span_q(jax.random.fold_in(streams_of[11], 71), 0)
    span_k = normal_values(streams_of[3], (PROMPTS, SPAN, KVH * HD), 1.0, 6.0, ((0, 64), (2, 8)))
    span_v = normal_values(streams_of[4], (PROMPTS, SPAN, KVH * HD), 1.0, 6.0, ((0, 64), (2, 8)))
    lengths = draw_lengths(jax.random.fold_in(streams_of[11], 71), 0)
    group_lists = draw_group_lists(jax.random.fold_in(streams_of[11], 71), 0)
    dec_q = draw_dec_q(jax.random.fold_in(streams_of[11], 71), 0)
    dec_k = draw_dec_k(jax.random.fold_in(streams_of[11], 71), 0)
    dec_v = normal_values(streams_of[9], (CANDS, STEPS, KVH * HD), 1.0, 6.0, ((0, 64), (2, 8)))
    out_weight = normal_values(streams_of[10], (QH * HD, D), (QH * HD) ** -0.5, 0.0625, ((0, 8), (1, 64)))
    return dict(ctx_keys=ctx_keys, ctx_values=ctx_values, span_q=span_q, span_k=span_k, span_v=span_v, lengths=lengths, group_lists=group_lists, dec_q=dec_q, dec_k=dec_k, dec_v=dec_v, out_weight=out_weight)


NEG = -1.0e30


def part_scores(query, keys):
    scale = float(query.shape[-1]) ** -0.5
    return jnp.einsum('rkgh,tkh->rkgt', query.astype(jnp.float32), keys.astype(jnp.float32)) * scale


def prompt_part(query, ctx_k, ctx_v, new_k, new_v, length, later):
    first = part_scores(query, ctx_k)
    second = part_scores(query, new_k)
    seen = (jnp.arange(ctx_k.shape[0]) < length)[None, None, None, :]
    top = jnp.maximum(jnp.max(jnp.where(seen, first, NEG), axis=-1), jnp.max(jnp.where(later, second, NEG), axis=-1))
    weight_one = jnp.where(seen, jnp.exp(first - top[..., None]), 0.0)
    weight_two = jnp.where(later, jnp.exp(second - top[..., None]), 0.0)
    total = jnp.sum(weight_one, axis=-1) + jnp.sum(weight_two, axis=-1)
    numer = jnp.einsum('rkgt,tkh->rkgh', weight_one.astype(jnp.bfloat16).astype(jnp.float32), ctx_v.astype(jnp.float32))
    numer = numer + jnp.einsum('rkgt,tkh->rkgh', weight_two.astype(jnp.bfloat16).astype(jnp.float32), new_v.astype(jnp.float32))
    return numer, top, total


def reference(ctx_keys, ctx_values, span_q, span_k, span_v, lengths, group_lists, dec_q, dec_k, dec_v, out_weight):
    group = QH // KVH

    def prefill_one(items):
        keys, values, query, new_k, new_v, length = items
        rows = query.shape[0]
        later = (jnp.arange(rows)[:, None] >= jnp.arange(rows)[None, :])[:, None, None, :]
        numer, top, total = prompt_part(query.reshape(rows, KVH, group, HD), keys.reshape(-1, KVH, HD), values.reshape(-1, KVH, HD), new_k.reshape(rows, KVH, HD), new_v.reshape(rows, KVH, HD), length, later)
        return (numer / total[..., None]).reshape(rows, QH * HD).astype(jnp.bfloat16)

    span_out = lax.map(prefill_one, (ctx_keys, ctx_values, span_q, span_k, span_v, lengths))
    prompt_ids = jnp.arange(PROMPTS, dtype=jnp.int32)

    def decode_one(cand):
        device = cand // CAND_DEV
        column = cand % CAND_DEV
        owner = jnp.sum(jnp.where(group_lists[:, column] == device, prompt_ids, 0)).astype(jnp.int32)
        keys = lax.dynamic_index_in_dim(ctx_keys, owner, 0, keepdims=False).reshape(-1, KVH, HD)
        values = lax.dynamic_index_in_dim(ctx_values, owner, 0, keepdims=False).reshape(-1, KVH, HD)
        new_k = lax.dynamic_index_in_dim(span_k, owner, 0, keepdims=False).reshape(-1, KVH, HD)
        new_v = lax.dynamic_index_in_dim(span_v, owner, 0, keepdims=False).reshape(-1, KVH, HD)
        length = lax.dynamic_index_in_dim(lengths, owner, 0, keepdims=False)
        query = lax.dynamic_index_in_dim(dec_q, cand, 0, keepdims=False).reshape(STEPS, KVH, group, HD)
        own_k = lax.dynamic_index_in_dim(dec_k, cand, 0, keepdims=False).reshape(STEPS, KVH, HD)
        own_v = lax.dynamic_index_in_dim(dec_v, cand, 0, keepdims=False).reshape(STEPS, KVH, HD)
        num_one, top_one, total_one = prompt_part(query, keys, values, new_k, new_v, length, True)
        third = part_scores(query, own_k)
        causal = (jnp.arange(STEPS)[:, None] >= jnp.arange(STEPS)[None, :])[:, None, None, :]
        top_two = jnp.max(jnp.where(causal, third, NEG), axis=-1)
        weight = jnp.where(causal, jnp.exp(third - top_two[..., None]), 0.0)
        total_two = jnp.sum(weight, axis=-1)
        num_two = jnp.einsum('rkgt,tkh->rkgh', weight.astype(jnp.bfloat16).astype(jnp.float32), own_v.astype(jnp.float32))
        top = jnp.maximum(top_one, top_two)
        factor_one = jnp.exp(top_one - top)
        factor_two = jnp.exp(top_two - top)
        mixed = (num_one * factor_one[..., None] + num_two * factor_two[..., None]) / (total_one * factor_one + total_two * factor_two)[..., None]
        return mixed.reshape(STEPS, QH * HD).astype(jnp.bfloat16)

    dec_out = lax.map(decode_one, jnp.arange(CANDS, dtype=jnp.int32))
    dec_proj = jnp.dot(dec_out.reshape(CANDS * STEPS, QH * HD), out_weight, preferred_element_type=jnp.float32)
    return span_out, dec_proj.reshape(CANDS, STEPS, D).astype(jnp.bfloat16)
```

```python
import math

import jax
import jax.numpy as jnp
from jax import lax
from jax.experimental import pallas as pl
from jax.experimental.pallas import tpu as pltpu
from jax.sharding import PartitionSpec as P

HD = 128
NX, NY, NZL, NZH = 4, 8, 2, 4
HEADS = 8
SPAN = 64
CHUNK = 1024
LOG2 = HD**-0.5 * math.log2(math.e)
NEG = -1e30
MESH = pl.DeviceIdType.MESH
NT = (((1,), (1,)), ((), ()))
TN = (((0,), (0,)), ((), ()))
NN = (((1,), (0,)), ((), ()))
NEAR = (0, 1, 7, 2, 6, 3, 5, 4)
NEAR_X = (1, 3, 2)


def dot(a, b, dims=NN):
    return lax.dot_general(a, b, dims, preferred_element_type=jnp.float32)


def iota(shape, dim):
    return lax.broadcasted_iota(jnp.int32, shape, dim)


def kernel(
    ck, cv, sq, sk, sv, length_ref, groups, dq, dk, dv, w_hbm,
    span_ref, proj_ref,
    k, v, svx, qs, m_s, acc_s, qf, kvf, g1, s2, r2, sel, msg, buf, w, pt, zs, rr,
    ksem, vsem, wsem, g1s, g1r, g2s, g2r, wss, wsr, p1s, p1r, p2s, p2r, cs, cr, rs, rrs,
):
    section, tp = lax.axis_index("section"), lax.axis_index("tp")
    zl, x, y = section // 32, lax.rem(section // NY, NX), lax.rem(section, NY)
    zh, core = tp // 2, lax.rem(tp, 2)
    block = section // NY

    def dev(sec, t):
        return {"section": sec, "tp": t}

    def remote(src, dst, ssem, rsem, device):
        return pltpu.make_async_remote_copy(
            src_ref=src, dst_ref=dst, send_sem=ssem, recv_sem=rsem, device_id=device, device_id_type=MESH
        )

    def yo(o):
        return lax.rem(y + o + NY, NY)

    def xo(o):
        return lax.rem(x + o + NX, NX)

    same = zl == core
    plane = core * 32 + x * NY
    turned = zh * 2 + zl

    barrier = pltpu.get_barrier_semaphore()

    def greet(device):
        pl.semaphore_signal(barrier, inc=1, device_id=device, device_id_type=MESH)

    for o in range(1, NY):
        greet(dev(block * NY + yo(o), tp))
    for o in range(1, NZL * NX):
        greet(dev(lax.rem(block + o, NZL * NX) * NY + y, tp))
    greet(dev(section, zh * 2 + 1 - core))

    @pl.when(jnp.logical_not(same))
    def _():
        for o in range(NY):
            greet(dev(plane + yo(o), turned))

    for zz in range(NZL):
        for hh in range(NZH):
            @pl.when(jnp.logical_not(jnp.logical_and(same, jnp.logical_and(zl == zz, zh == hh))))
            def _(zz=zz, hh=hh):
                greet(dev(zz * 32 + x * NY + y, hh * 2 + zl))

    nch = ck.shape[1] // CHUNK
    copies = []
    for i in range(nch):
        rows = pl.ds(i * CHUNK, CHUNK)
        a = pltpu.make_async_copy(ck.at[0, rows], k.at[rows], ksem.at[i])
        b = pltpu.make_async_copy(cv.at[0, rows], v.at[rows, pl.ds(0, HD)], vsem.at[i])
        a.start()
        b.start()
        copies.append((a, b))

    for j in range(4):
        piece = dq[j].astype(jnp.float32)
        for h in range(HEADS):
            qf[pl.ds(j * 16 + h, 2, stride=8), :] = piece[:, h * HD:(h + 1) * HD]
        kvf[2 * j:2 * j + 2, :] = dk[j].astype(jnp.float32)
        kvf[8 + 2 * j:10 + 2 * j, :] = dv[j].astype(jnp.float32)
    g1[y, 0:64, :] = qf[...].astype(jnp.bfloat16)
    g1[y, 64:80, :] = kvf[...].astype(jnp.bfloat16)

    for h in range(HEADS):
        qs[h * SPAN:(h + 1) * SPAN, :] = sq[0, :, h * HD:(h + 1) * HD]
    svx[:, 0:HD] = sv[0]
    svx[:, HD:] = jnp.ones((SPAN, HD), jnp.bfloat16)
    n_rows = HEADS * SPAN
    first = dot(qs[...], sk[0], NT)
    shape = (n_rows, SPAN)
    first = jnp.where(iota(shape, 1) <= (iota(shape, 0) & (SPAN - 1)), first, NEG)
    top = jnp.max(first, axis=1, keepdims=True) * LOG2
    weights = jnp.exp2(first * LOG2 - top)
    acc_s[...] = dot(weights.astype(jnp.bfloat16), svx[...])
    m_s[...] = jnp.broadcast_to(top, m_s.shape)
    length = length_ref[0]

    def span_chunk(i):
        copies[i][0].wait()
        copies[i][1].wait()
        rows = pl.ds(i * CHUNK, CHUNK)
        seen = jnp.where(iota((CHUNK, HD), 0) + i * CHUNK < length, 1.0, 0.0).astype(jnp.bfloat16)
        kc = k[rows, :] * seen + k[0:1, :] * (1 - seen)
        k[rows, :] = kc
        v[rows, 0:HD] = v[rows, 0:HD] * seen
        v[rows, HD:] = seen
        s = dot(qs[...], kc, NT)
        old = m_s[...]
        new = jnp.maximum(old, jnp.max(s, axis=1, keepdims=True) * LOG2)
        p = jnp.exp2(s * LOG2 - new[:, 0:1])
        shrink = jnp.exp2(old - new)
        m_s[...] = new
        part = dot(p.astype(jnp.bfloat16), v[rows, :])
        acc_s[:, 0:HD] = acc_s[:, 0:HD] * shrink + part[:, 0:HD]
        acc_s[:, HD:] = acc_s[:, HD:] * shrink + part[:, HD:]

    for i in range(0, 2):
        span_chunk(i)

    pl.semaphore_wait(
        barrier, (NY - 1) + (NZL * NX - 1) + 1 + jnp.where(same, NZL * NZH - 1, NY + NZL * NZH)
    )

    sent = []
    for o in NEAR[1:]:
        c = remote(g1.at[y], g1.at[y], g1s.at[o], g1r.at[o], dev(block * NY + yo(o), tp))
        c.start()
        sent.append(c)
    w_copy = pltpu.make_async_copy(w_hbm, w, wsem)
    w_swap = remote(w_hbm, w, wss, wsr, dev(plane + y, turned))

    @pl.when(same)
    def _():
        w_copy.start()

    @pl.when(jnp.logical_not(same))
    def _():
        w_swap.start()

    for i in range(2, nch):
        span_chunk(i)

    for h in range(HEADS):
        rows = slice(h * SPAN, (h + 1) * SPAN)
        span_ref[0, :, h * HD:(h + 1) * HD] = (acc_s[rows, 0:HD] / acc_s[rows, HD:]).astype(jnp.bfloat16)

    for o in NEAR[1:]:
        slot = yo(-o)
        remote(g1.at[slot], g1.at[slot], g1s.at[o], g1r.at[o], dev(block * NY + yo(o), tp)).wait_recv()

    owner_of = (iota((16, HD), 0) & 7) // 2
    sent2 = []
    for o in (1, 7, 2, 6, 3, 5, 4, 0):
        to = lax.rem(block + o, NZL * NX)
        own = jnp.zeros((16, HD), jnp.float32)
        for j in range(4):
            at = groups[to * NY + y, j] & (NY - 1)
            s2[to, j * 16:(j + 1) * 16, :] = g1[at, j * 16:(j + 1) * 16, :]
            own = jnp.where(owner_of == j, g1[at, 64:80, :].astype(jnp.float32), own)
        s2[to, 64:80, :] = own.astype(jnp.bfloat16)
        if o:
            c = remote(s2.at[to], r2.at[block], g2s.at[o], g2r.at[o], dev(to * NY + y, tp))
            c.start()
            sent2.append(c)
    r2[block] = s2[block]

    lane = iota((16, 512), 1)
    sub = iota((16, 512), 0)
    col = (sub & 7) // 2

    def one_hot(i, _):
        want = jnp.zeros((16, 512), jnp.int32)
        for half in range(2):
            for j in range(4):
                want = jnp.where(
                    jnp.logical_and(sub // 8 == half, col == j), groups[2 * i + half, j], want
                )
        hit = want * 8 + (sub & 7) == lane
        pt[pl.ds(pl.multiple_of(i * 16, 16), 16), :] = jnp.where(hit, 1.0, 0.0).astype(jnp.bfloat16)
        return 0

    lax.fori_loop(0, 32, one_hot, 0)

    for o in range(1, NZL * NX):
        slot = lax.rem(block + NZL * NX - o, NZL * NX)
        remote(s2.at[slot], r2.at[slot], g2s.at[o], g2r.at[o], dev(slot * NY + y, tp)).wait_recv()
    own = jnp.zeros((16, HD), jnp.float32)
    for j in range(4):
        at = lax.shift_right_logical(groups[section, j], 3)
        qf[j * 16:(j + 1) * 16, :] = r2[at, j * 16:(j + 1) * 16, :].astype(jnp.float32)
        own = jnp.where(owner_of == j, r2[at, 64:80, :].astype(jnp.float32), own)

    for h in range(0, HEADS, 2):
        pair = [qf[pl.ds(h + e, 8, stride=8), :] for e in range(2)]
        sel[h * 8:h * 8 + 16, :] = jnp.concatenate(pair, axis=0).astype(jnp.bfloat16)
    query = sel[...]
    own_k = own.astype(jnp.bfloat16)
    own_v = jnp.concatenate([own[8:16], own[0:8]], axis=0).astype(jnp.bfloat16)
    own_v = jnp.concatenate([own_v, jnp.ones((16, HD), jnp.bfloat16)], axis=1)
    s_ctx = dot(query, k[...], NT)
    s_blk = dot(query, sk[0], NT)
    s_own = dot(query, own_k, NT)
    r16, c16 = iota((64, 16), 0), iota((64, 16), 1)
    fits = jnp.logical_and(c16 // 2 == (r16 // 2) % 4, c16 % 2 <= r16 % 2)
    s_own = jnp.where(fits, s_own, NEG)
    top = jnp.maximum(
        jnp.maximum(jnp.max(s_ctx, axis=1, keepdims=True), jnp.max(s_blk, axis=1, keepdims=True)),
        jnp.max(s_own, axis=1, keepdims=True),
    ) * LOG2
    total = dot(jnp.exp2(s_ctx * LOG2 - top).astype(jnp.bfloat16), v[...])
    total += dot(jnp.exp2(s_blk * LOG2 - top).astype(jnp.bfloat16), svx[...])
    total += dot(jnp.exp2(s_own * LOG2 - top).astype(jnp.bfloat16), own_v)
    msg[...] = (total[:, 0:HD] / total[:, HD:]).astype(jnp.bfloat16)

    sent3 = []
    for o in NEAR:
        c = remote(msg, buf.at[section], p1s.at[o], p1r.at[o], dev(plane + yo(o), turned))
        if o:
            c.start()
            sent3.append(c)
        else:
            pl.when(jnp.logical_not(same))(c.start)

            @pl.when(same)
            def _():
                buf[section] = msg[...]

    def sibling(slot, i):
        return remote(buf.at[slot], buf.at[slot], cs.at[i], cr.at[i], dev(section, zh * 2 + 1 - core))

    for o in NEAR:
        slot = plane + yo(-o)
        c = remote(msg, buf.at[slot], p1s.at[o], p1r.at[o], dev(plane + yo(o), turned))
        if o:
            c.wait_recv()
        else:
            pl.when(jnp.logical_not(same))(c.wait_recv)
        for d in NEAR_X:
            c = remote(
                buf.at[slot], buf.at[slot], p2s.at[o, d], p2r.at[o, d],
                dev(zl * 32 + xo(d) * NY + y, tp),
            )
            c.start()
            sent3.append(c)
        c = sibling(slot, o * 4)
        c.start()
        sent3.append(c)
    for o in NEAR:
        for d in NEAR_X:
            slot = core * 32 + xo(-d) * NY + yo(-o)
            remote(
                buf.at[slot], buf.at[slot], p2s.at[o, d], p2r.at[o, d],
                dev(zl * 32 + xo(d) * NY + y, tp),
            ).wait_recv()
            c = sibling(slot, o * 4 + d)
            c.start()
            sent3.append(c)
    for o in NEAR:
        for d in (0, *NEAR_X):
            slot = (1 - core) * 32 + xo(-d) * NY + yo(-o)
            sibling(slot, o * 4 + d).wait_recv()

    pl.when(same)(w_copy.wait)
    pl.when(jnp.logical_not(same))(w_swap.wait_recv)
    full = None
    for pair in range(HEADS // 2):
        at = pair * 2 * HD
        both = jnp.concatenate([w[at:at + HD, :], w[at + HD:at + 2 * HD, :]], axis=1)
        part = dot(buf[:, pair * 16:(pair + 1) * 16, :].reshape(1024, HD), both)
        full = part if full is None else full + part
    full = full.reshape(64, 16, 2 * HD)
    rows = (full[:, 0:8, 0:HD] + full[:, 8:16, HD:]).reshape(512, HD).astype(jnp.bfloat16)
    zs[...] = dot(pt[...], rows, TN).astype(jnp.bfloat16)

    sent4 = []
    for t in range(8):
        c = remote(
            zs.at[pl.ds(t * 64, 64)], rr.at[turned], rs.at[t], rrs.at[turned], dev(plane + y, t)
        )
        mine = jnp.logical_and(same, tp == t)
        pl.when(jnp.logical_not(mine))(c.start)

        @pl.when(mine)
        def _(t=t):
            rr[turned] = zs[t * 64:(t + 1) * 64, :]

        sent4.append((c, mine))
    out = None
    for s in range(8):
        c = remote(zs.at[pl.ds(s * 64, 64)], rr.at[s], rs.at[s], rrs.at[s], dev(plane + y, s))
        pl.when(jnp.logical_not(jnp.logical_and(same, turned == s)))(c.wait_recv)
    for s in range(8):
        part = rr[s].astype(jnp.float32)
        out = part if out is None else out + part
    proj_ref[...] = out.astype(jnp.bfloat16)

    for c in sent + sent2 + sent3:
        c.wait_send()
    pl.when(jnp.logical_not(same))(w_swap.wait_send)
    c = remote(msg, buf.at[section], p1s.at[0], p1r.at[0], dev(plane + y, turned))
    pl.when(jnp.logical_not(same))(c.wait_send)
    for c, mine in sent4:
        pl.when(jnp.logical_not(mine))(c.wait_send)


def body(ctx_keys, ctx_values, span_q, span_k, span_v, lengths, group_lists, dec_q, dec_k, dec_v, out_weight):
    ctx = ctx_keys.shape[1]
    bf, f32 = jnp.bfloat16, jnp.float32
    vmem = pl.BlockSpec(memory_space=pltpu.VMEM)
    smem = pl.BlockSpec(memory_space=pltpu.SMEM)
    hbm = pl.BlockSpec(memory_space=pltpu.HBM)
    dma = pltpu.SemaphoreType.DMA
    span_out, proj = pl.pallas_call(
        kernel,
        name="block_and_decode_attention",
        out_shape=(
            jax.ShapeDtypeStruct(span_q.shape, bf),
            jax.ShapeDtypeStruct((64, HD), bf),
        ),
        in_specs=[hbm, hbm, vmem, vmem, vmem, smem, smem, vmem, vmem, vmem, hbm],
        out_specs=(vmem, vmem),
        scratch_shapes=[
            pltpu.VMEM((ctx, HD), bf),
            pltpu.VMEM((ctx, 2 * HD), bf),
            pltpu.VMEM((SPAN, 2 * HD), bf),
            pltpu.VMEM((HEADS * SPAN, HD), bf),
            pltpu.VMEM((HEADS * SPAN, HD), f32),
            pltpu.VMEM((HEADS * SPAN, 2 * HD), f32),
            pltpu.VMEM((64, HD), f32),
            pltpu.VMEM((16, HD), f32),
            pltpu.VMEM((8, 80, HD), bf),
            pltpu.VMEM((8, 80, HD), bf),
            pltpu.VMEM((8, 80, HD), bf),
            pltpu.VMEM((64, HD), bf),
            pltpu.VMEM((64, HD), bf),
            pltpu.VMEM((64, 64, HD), bf),
            pltpu.VMEM((HEADS * HD, HD), bf),
            pltpu.VMEM((512, 512), bf),
            pltpu.VMEM((512, HD), bf),
            pltpu.VMEM((8, 64, HD), bf),
            dma((ctx // CHUNK,)), dma((ctx // CHUNK,)), dma,
            dma((8,)), dma((8,)), dma((8,)), dma((8,)), dma, dma,
            dma((8,)), dma((8,)), dma((8, 4)), dma((8, 4)), dma((32,)), dma((32,)),
            dma((8,)), dma((8,)),
        ],
        compiler_params=pltpu.CompilerParams(
            collective_id=0, has_side_effects=True, vmem_limit_bytes=48 << 20
        ),
        cost_estimate=pl.CostEstimate(flops=2_000_000_000, bytes_accessed=4 << 20, transcendentals=3_600_000),
    )(
        ctx_keys, ctx_values, span_q, span_k, span_v, lengths, group_lists, dec_q, dec_k, dec_v, out_weight
    )
    return span_out, proj.reshape(32, 2, HD)


def solution(mesh):
    in_specs = (
        P("section", None, "tp"),
        P("section", None, "tp"),
        P("section", None, "tp"),
        P("section", None, "tp"),
        P("section", None, "tp"),
        P("section"),
        P(),
        P("section", None, "tp"),
        P("section", None, "tp"),
        P("section", None, "tp"),
        P("tp", "section"),
    )
    out_specs = (P("section", None, "tp"), P("tp", None, "section"))
    return jax.shard_map(body, mesh=mesh, in_specs=in_specs, out_specs=out_specs, check_vma=False)
```

```python
import functools
import math

import jax
import jax.numpy as jnp
from jax import lax
from jax.experimental import pallas as pl
from jax.experimental.pallas import tpu as pltpu
from jax.sharding import PartitionSpec as P

HD = 128
NX, NY, NZL, NZH = 4, 8, 2, 4
HEADS = 8
SPAN = 64
CHUNK = 1024
LOG2 = HD**-0.5 * math.log2(math.e)
NEG = -1e30
MESH = pl.DeviceIdType.MESH
NT = (((1,), (1,)), ((), ()))
TN = (((0,), (0,)), ((), ()))
NN = (((1,), (0,)), ((), ()))
NEAR = (0, 1, 7, 2, 6, 3, 5, 4)
NEAR_X = (1, 3, 2)
FAR = (4, 3, 5, 2, 6, 1, 7)


def dot(a, b, dims=NN):
    return lax.dot_general(a, b, dims, preferred_element_type=jnp.float32)


def iota(shape, dim):
    return lax.broadcasted_iota(jnp.int32, shape, dim)


def kernel(
    length_ref, ck, cv, sq_hbm, sk_hbm, sv_hbm, groups_hbm, dq_hbm, dk_hbm, dv_hbm, w_hbm,
    span_ref, proj_ref,
    sq, sk, svx, groups, dq, dk, dv, insem,
    k, v, qs, m_s, acc_s, qf, kvf, g1, s2, r2, sel, msg, buf, w, pt, zp, zs, rr,
    ksem, vsem, wsem, g1s, g1r, g2s, g2r, wss, wsr, p1s, p1r, p2s, p2r, cs, cr, rs, rrs,
):
    section, tp = lax.axis_index("section"), lax.axis_index("tp")
    zl, x, y = section // 32, lax.rem(section // NY, NX), lax.rem(section, NY)
    zh, core = tp // 2, lax.rem(tp, 2)
    block = section // NY

    def dev(sec, t):
        return {"section": sec, "tp": t}

    def remote(src, dst, ssem, rsem, device):
        return pltpu.make_async_remote_copy(
            src_ref=src, dst_ref=dst, send_sem=ssem, recv_sem=rsem, device_id=device, device_id_type=MESH
        )

    def yo(o):
        return lax.rem(y + o + NY, NY)

    def xo(o):
        return lax.rem(x + o + NX, NX)

    same = zl == core
    buf4 = buf.reshape(NZL, NX, NY, 64, HD)
    plane = core * 32 + x * NY
    turned = zh * 2 + zl

    small = []
    for i, (src, dst) in enumerate((
        (dq_hbm, dq), (dk_hbm, dk), (dv_hbm, dv), (sq_hbm.at[0], sq), (sk_hbm.at[0], sk),
        (sv_hbm.at[0], svx.at[:, pl.ds(0, HD)]), (groups_hbm, groups),
    )):
        c = pltpu.make_async_copy(src, dst, insem.at[i])
        c.start()
        small.append(c)

    barrier = pltpu.get_barrier_semaphore()

    def greet(device):
        pl.semaphore_signal(barrier, inc=1, device_id=device, device_id_type=MESH)

    for o in range(1, NY):
        greet(dev(block * NY + yo(o), tp))
    for o in range(1, NZL * NX):
        greet(dev(lax.rem(block + o, NZL * NX) * NY + y, tp))
    greet(dev(section, zh * 2 + 1 - core))

    @pl.when(jnp.logical_not(same))
    def _():
        for o in range(NY):
            greet(dev(plane + yo(o), turned))

    for zz in range(NZL):
        for hh in range(NZH):
            @pl.when(jnp.logical_not(jnp.logical_and(same, jnp.logical_and(zl == zz, zh == hh))))
            def _(zz=zz, hh=hh):
                greet(dev(zz * 32 + x * NY + y, hh * 2 + zl))

    nch = ck.shape[1] // CHUNK

    def chunk_copies(i):
        rows = pl.ds(i * CHUNK, CHUNK)
        return (
            pltpu.make_async_copy(ck.at[0, rows], k.at[rows], ksem.at[i]),
            pltpu.make_async_copy(cv.at[0, rows], v.at[rows, pl.ds(0, HD)], vsem.at[i]),
        )

    for i in range(nch):
        for c in chunk_copies(i):
            c.start()

    for c in small[:3]:
        c.wait()
    for j in range(4):
        piece = dq[j].astype(jnp.float32)
        for h in range(HEADS):
            qf[pl.ds(j * 16 + h, 2, stride=8), :] = piece[:, h * HD:(h + 1) * HD]
        kvf[2 * j:2 * j + 2, :] = dk[j].astype(jnp.float32)
        kvf[8 + 2 * j:10 + 2 * j, :] = dv[j].astype(jnp.float32)
    g1[y, 0:64, :] = qf[...].astype(jnp.bfloat16)
    g1[y, 64:80, :] = kvf[...].astype(jnp.bfloat16)

    pl.semaphore_wait(
        barrier, (NY - 1) + (NZL * NX - 1) + 1 + jnp.where(same, NZL * NZH - 1, NY + NZL * NZH)
    )

    sent = []
    for o in FAR:
        c = remote(g1.at[y], g1.at[y], g1s.at[o], g1r.at[o], dev(block * NY + yo(o), tp))
        c.start()
        sent.append(c)
    w_copy = pltpu.make_async_copy(w_hbm, w, wsem)
    w_swap = remote(w_hbm, w, wss, wsr, dev(plane + y, turned))

    @pl.when(same)
    def _():
        w_copy.start()

    @pl.when(jnp.logical_not(same))
    def _():
        w_swap.start()

    for c in small[3:]:
        c.wait()
    for h in range(HEADS):
        qs[h * SPAN:(h + 1) * SPAN, :] = sq[:, h * HD:(h + 1) * HD]
    svx[:, HD:] = jnp.ones((SPAN, HD), jnp.bfloat16)
    n_rows = HEADS * SPAN
    first = dot(qs[...], sk[...], NT)
    shape = (n_rows, SPAN)
    first = jnp.where(iota(shape, 1) <= (iota(shape, 0) & (SPAN - 1)), first, NEG)
    top = jnp.max(first, axis=1, keepdims=True) * LOG2
    weights = jnp.exp2(first * LOG2 - top)
    acc_s[...] = dot(weights.astype(jnp.bfloat16), svx[...])
    m_s[...] = jnp.broadcast_to(top, m_s.shape)
    length = length_ref[0]

    def span_chunk(i):
        rows = pl.ds(i * CHUNK, CHUNK)
        for c in chunk_copies(i):
            c.wait()
        seen = jnp.where(iota((CHUNK, HD), 0) + i * CHUNK < length, 1.0, 0.0).astype(jnp.bfloat16)
        kc = k[rows, :] * seen + k[0:1, :] * (1 - seen)
        k[rows, :] = kc
        v[rows, 0:HD] = v[rows, 0:HD] * seen
        v[rows, HD:] = seen
        s = dot(qs[...], kc, NT)
        old = m_s[...]
        new = jnp.maximum(old, jnp.max(s, axis=1, keepdims=True) * LOG2)
        p = jnp.exp2(s * LOG2 - new[:, 0:1])
        shrink = jnp.exp2(old - new)
        m_s[...] = new
        part = dot(p.astype(jnp.bfloat16), v[rows, :])
        acc_s[:, 0:HD] = acc_s[:, 0:HD] * shrink + part[:, 0:HD]
        acc_s[:, HD:] = acc_s[:, HD:] * shrink + part[:, HD:]

    for i in range(nch - 1):
        span_chunk(i)

    for o in NEAR[1:]:
        slot = yo(-o)
        remote(g1.at[slot], g1.at[slot], g1s.at[o], g1r.at[o], dev(block * NY + yo(o), tp)).wait_recv()

    owner_of = (iota((16, HD), 0) & 7) // 2
    sent2 = []
    for o in (6, 2, 5, 7, 1, 3, 4, 0):
        to = lax.rem(block + o, NZL * NX)
        own = jnp.zeros((16, HD), jnp.float32)
        for j in range(4):
            at = groups[j, to * NY + y] & (NY - 1)
            s2[to, j * 16:(j + 1) * 16, :] = g1[at, j * 16:(j + 1) * 16, :]
            own = jnp.where(owner_of == j, g1[at, 64:80, :].astype(jnp.float32), own)
        s2[to, 64:80, :] = own.astype(jnp.bfloat16)
        if o:
            c = remote(s2.at[to], r2.at[block], g2s.at[o], g2r.at[o], dev(to * NY + y, tp))
            c.start()
            sent2.append(c)
    r2[block] = s2[block]

    span_chunk(nch - 1)

    for o in range(1, NZL * NX):
        slot = lax.rem(block + NZL * NX - o, NZL * NX)
        remote(s2.at[slot], r2.at[slot], g2s.at[o], g2r.at[o], dev(slot * NY + y, tp)).wait_recv()
    own = jnp.zeros((16, HD), jnp.float32)
    for j in range(4):
        at = lax.shift_right_logical(groups[j, section], 3)
        qf[j * 16:(j + 1) * 16, :] = r2[at, j * 16:(j + 1) * 16, :].astype(jnp.float32)
        own = jnp.where(owner_of == j, r2[at, 64:80, :].astype(jnp.float32), own)

    for h in range(0, HEADS, 2):
        pair = [qf[pl.ds(h + e, 8, stride=8), :] for e in range(2)]
        sel[h * 8:h * 8 + 16, :] = jnp.concatenate(pair, axis=0).astype(jnp.bfloat16)
    query = sel[...]
    own_k = own.astype(jnp.bfloat16)
    own_v = jnp.concatenate([own[8:16], own[0:8]], axis=0).astype(jnp.bfloat16)
    own_v = jnp.concatenate([own_v, jnp.ones((16, HD), jnp.bfloat16)], axis=1)
    s_ctx = dot(query, k[...], NT)
    s_blk = dot(query, sk[...], NT)
    s_own = dot(query, own_k, NT)
    r16, c16 = iota((64, 16), 0), iota((64, 16), 1)
    fits = jnp.logical_and(c16 // 2 == (r16 // 2) % 4, c16 % 2 <= r16 % 2)
    s_own = jnp.where(fits, s_own, NEG)
    top = jnp.maximum(
        jnp.maximum(jnp.max(s_ctx, axis=1, keepdims=True), jnp.max(s_blk, axis=1, keepdims=True)),
        jnp.max(s_own, axis=1, keepdims=True),
    ) * LOG2
    total = dot(jnp.exp2(s_ctx * LOG2 - top).astype(jnp.bfloat16), v[...])
    total += dot(jnp.exp2(s_blk * LOG2 - top).astype(jnp.bfloat16), svx[...])
    total += dot(jnp.exp2(s_own * LOG2 - top).astype(jnp.bfloat16), own_v)
    msg[...] = (total[:, 0:HD] / total[:, HD:]).astype(jnp.bfloat16)

    sent3 = []
    for o in NEAR:
        c = remote(msg, buf.at[section], p1s.at[o], p1r.at[o], dev(plane + yo(o), turned))
        if o:
            c.start()
            sent3.append(c)
        else:
            pl.when(jnp.logical_not(same))(c.start)

            @pl.when(same)
            def _():
                buf[section] = msg[...]

    for h in range(HEADS):
        rows = slice(h * SPAN, (h + 1) * SPAN)
        span_ref[0, :, h * HD:(h + 1) * HD] = (acc_s[rows, 0:HD] / acc_s[rows, HD:]).astype(jnp.bfloat16)

    lane = iota((16, 512), 1)
    sub = iota((16, 512), 0)
    col = (sub & 7) // 2

    def one_hot(i, _):
        want = jnp.zeros((16, 512), jnp.int32)
        for half in range(2):
            for j in range(4):
                want = jnp.where(
                    jnp.logical_and(sub // 8 == half, col == j), groups[j, 2 * i + half], want
                )
        hit = ((want * 8 + (sub & 7) + (NZH - zh) * 128) & 511) == lane
        pt[pl.ds(pl.multiple_of(i * 16, 16), 16), :] = jnp.where(hit, 1.0, 0.0).astype(jnp.bfloat16)
        return 0

    lax.fori_loop(0, 32, one_hot, 0)

    def sibling(half, o):
        part = buf4.at[half, :, yo(-o)]
        return remote(part, part, cs.at[o], cr.at[o], dev(section, zh * 2 + 1 - core))

    for o in NEAR:
        slot = plane + yo(-o)
        c = remote(msg, buf.at[slot], p1s.at[o], p1r.at[o], dev(plane + yo(o), turned))
        if o:
            c.wait_recv()
        else:
            pl.when(jnp.logical_not(same))(c.wait_recv)
        for d in (2, 1, 3):
            c = remote(
                buf.at[slot], buf.at[slot], p2s.at[o, d], p2r.at[o, d],
                dev(zl * 32 + xo(d) * NY + y, tp),
            )
            c.start()
            sent3.append(c)
    for o in NEAR:
        for d in NEAR_X:
            slot = core * 32 + xo(-d) * NY + yo(-o)
            remote(
                buf.at[slot], buf.at[slot], p2s.at[o, d], p2r.at[o, d],
                dev(zl * 32 + xo(d) * NY + y, tp),
            ).wait_recv()
        c = sibling(core, o)
        c.start()
        sent3.append(c)
    pl.when(same)(w_copy.wait)
    pl.when(jnp.logical_not(same))(w_swap.wait_recv)

    def project(half):
        full = None
        for pair in range(HEADS // 2):
            at = pair * 2 * HD
            both = jnp.concatenate([w[at:at + HD, :], w[at + HD:at + 2 * HD, :]], axis=1)
            x_pair = buf[pl.ds(half * 32, 32), pair * 16:(pair + 1) * 16, :].reshape(512, HD)
            part = dot(x_pair, both)
            full = part if full is None else full + part
        full = full.reshape(32, 16, 2 * HD)
        rows = (full[:, 0:8, 0:HD] + full[:, 8:16, HD:]).reshape(256, HD)
        zp[pl.ds(pl.multiple_of(half * 256, 256), 256), :] = rows.astype(jnp.bfloat16)

    project(core)
    for o in NEAR:
        sibling(1 - core, o).wait_recv()
    project(1 - core)

    sent4 = []
    for hh in (2, 1, 3, 0):
        rows = dot(pt[:, hh * 128:(hh + 1) * 128], zp[...], TN)
        zs[hh * 128:(hh + 1) * 128, :] = rows.astype(jnp.bfloat16)
        for e in range(2):
            at = pl.ds(hh * 128 + e * 64, 64)
            to = lax.rem(zh + hh, NZH) * 2 + e
            c = remote(zs.at[at], rr.at[turned], rs.at[hh * 2 + e], rrs.at[turned], dev(plane + y, to))
            if hh:
                c.start()
                sent4.append(c.wait_send)
                continue
            mine = jnp.logical_and(same, core == e)
            other = jnp.logical_not(mine)
            pl.when(other)(c.start)
            sent4.append(functools.partial(pl.when(other), c.wait_send))

            @pl.when(mine)
            def _():
                rr[turned] = zs[at, :]

    out = None
    for s in range(8):
        c = remote(zs.at[pl.ds(s * 64, 64)], rr.at[s], rs.at[s], rrs.at[s], dev(plane + y, s))
        pl.when(jnp.logical_not(jnp.logical_and(same, turned == s)))(c.wait_recv)
    for s in range(8):
        part = rr[s].astype(jnp.float32)
        out = part if out is None else out + part
    proj_ref[...] = out.astype(jnp.bfloat16)

    for c in sent + sent2 + sent3:
        c.wait_send()
    pl.when(jnp.logical_not(same))(w_swap.wait_send)
    c = remote(msg, buf.at[section], p1s.at[0], p1r.at[0], dev(plane + y, turned))
    pl.when(jnp.logical_not(same))(c.wait_send)
    for wait in sent4:
        wait()


def body(ctx_keys, ctx_values, span_q, span_k, span_v, lengths, group_lists, dec_q, dec_k, dec_v, out_weight):
    ctx = ctx_keys.shape[1]
    bf, f32 = jnp.bfloat16, jnp.float32
    vmem = pl.BlockSpec(memory_space=pltpu.VMEM)
    hbm = pl.BlockSpec(memory_space=pl.ANY)
    dma = pltpu.SemaphoreType.DMA
    span_out, proj = pl.pallas_call(
        kernel,
        name="block_and_decode_attention",
        out_shape=(
            pltpu.VMEM(span_q.shape, bf),
            pltpu.VMEM((64, HD), bf),
        ),
        in_specs=[pl.BlockSpec(memory_space=pltpu.SMEM)] + [hbm] * 10,
        out_specs=(vmem, vmem),
        scratch_shapes=[
            pltpu.VMEM((SPAN, HEADS * HD), bf),
            pltpu.VMEM((SPAN, HD), bf),
            pltpu.VMEM((SPAN, 2 * HD), bf),
            pltpu.SMEM((4, 64), jnp.int32),
            pltpu.VMEM(dec_q.shape, bf),
            pltpu.VMEM(dec_k.shape, bf),
            pltpu.VMEM(dec_v.shape, bf),
            dma((8,)),
            pltpu.VMEM((ctx, HD), bf),
            pltpu.VMEM((ctx, 2 * HD), bf),
            pltpu.VMEM((HEADS * SPAN, HD), bf),
            pltpu.VMEM((HEADS * SPAN, HD), f32),
            pltpu.VMEM((HEADS * SPAN, 2 * HD), f32),
            pltpu.VMEM((64, HD), f32),
            pltpu.VMEM((16, HD), f32),
            pltpu.VMEM((8, 80, HD), bf),
            pltpu.VMEM((8, 80, HD), bf),
            pltpu.VMEM((8, 80, HD), bf),
            pltpu.VMEM((64, HD), bf),
            pltpu.VMEM((64, HD), bf),
            pltpu.VMEM((64, 64, HD), bf),
            pltpu.VMEM((HEADS * HD, HD), bf),
            pltpu.VMEM((512, 512), bf),
            pltpu.VMEM((512, HD), bf),
            pltpu.VMEM((512, HD), bf),
            pltpu.VMEM((8, 64, HD), bf),
            dma((ctx // CHUNK,)), dma((ctx // CHUNK,)), dma,
            dma((8,)), dma((8,)), dma((8,)), dma((8,)), dma, dma,
            dma((8,)), dma((8,)), dma((8, 4)), dma((8, 4)), dma((8,)), dma((8,)),
            dma((8,)), dma((8,)),
        ],
        compiler_params=pltpu.CompilerParams(
            collective_id=0, has_side_effects=True, vmem_limit_bytes=58 << 20
        ),
        cost_estimate=pl.CostEstimate(flops=2_000_000_000, bytes_accessed=4 << 20, transcendentals=3_600_000),
    )(
        lengths,
        *(
            pltpu.with_memory_space_constraint(a, pltpu.HBM)
            for a in (
                ctx_keys, ctx_values, span_q, span_k, span_v, group_lists.T, dec_q, dec_k, dec_v, out_weight
            )
        ),
    )
    return span_out, proj.reshape(32, 2, HD)


def solution(mesh):
    in_specs = (
        P("section", None, "tp"),
        P("section", None, "tp"),
        P("section", None, "tp"),
        P("section", None, "tp"),
        P("section", None, "tp"),
        P("section"),
        P(),
        P("section", None, "tp"),
        P("section", None, "tp"),
        P("section", None, "tp"),
        P("tp", "section"),
    )
    out_specs = (P("section", None, "tp"), P("tp", None, "section"))
    return jax.shard_map(body, mesh=mesh, in_specs=in_specs, out_specs=out_specs, check_vma=False)
```

```python
import functools
import math

import jax
import jax.numpy as jnp
from jax import lax
from jax.experimental import pallas as pl
from jax.experimental.pallas import tpu as pltpu
from jax.sharding import PartitionSpec as P

HD = 128
NX, NY, NZL, NZH = 4, 8, 2, 4
HEADS = 8
SPAN = 64
CHUNK = 1024
LOG2 = HD**-0.5 * math.log2(math.e)
NEG = -1e30
MESH = pl.DeviceIdType.MESH
NT = (((1,), (1,)), ((), ()))
TN = (((0,), (0,)), ((), ()))
NN = (((1,), (0,)), ((), ()))
NEAR = (0, 1, 7, 2, 6, 3, 5, 4)
NEAR_X = (1, 3, 2)
FAR = (4, 3, 5, 2, 6, 1, 7)


def dot(a, b, dims=NN):
    return lax.dot_general(a, b, dims, preferred_element_type=jnp.float32)


def iota(shape, dim):
    return lax.broadcasted_iota(jnp.int32, shape, dim)


def kernel(
    length_ref, ck, cv, sq_hbm, sk_hbm, sv_hbm, groups_hbm, dq_hbm, dk_hbm, dv_hbm, w_hbm,
    span_ref, proj_ref,
    sq, sk, svx, groups, dq, dk, dv, insem,
    k, v, qs, m_s, acc_s, qf, kvf, g1, s2, r2, sel, msg, buf, w, pt, zp, zs, rr,
    ksem, vsem, wsem, g1s, g1r, g2s, g2r, wss, wsr, p1s, p1r, p2s, p2r, cs, cr, rs, rrs,
):
    section, tp = lax.axis_index("section"), lax.axis_index("tp")
    zl, x, y = section // 32, lax.rem(section // NY, NX), lax.rem(section, NY)
    zh, core = tp // 2, lax.rem(tp, 2)
    block = section // NY

    def dev(sec, t):
        return {"section": sec, "tp": t}

    def remote(src, dst, ssem, rsem, device):
        return pltpu.make_async_remote_copy(
            src_ref=src, dst_ref=dst, send_sem=ssem, recv_sem=rsem, device_id=device, device_id_type=MESH
        )

    def yo(o):
        return lax.rem(y + o + NY, NY)

    def xo(o):
        return lax.rem(x + o + NX, NX)

    same = zl == core
    buf4 = buf.reshape(NZL, NX, NY, 64, HD)
    plane = core * 32 + x * NY
    turned = zh * 2 + zl

    small = []
    for i, (src, dst) in enumerate((
        (dq_hbm, dq), (dk_hbm, dk), (dv_hbm, dv), (sq_hbm.at[0], sq), (sk_hbm.at[0], sk),
        (sv_hbm.at[0], svx.at[:, pl.ds(0, HD)]), (groups_hbm, groups),
    )):
        c = pltpu.make_async_copy(src, dst, insem.at[i])
        c.start()
        small.append(c)

    barrier = pltpu.get_barrier_semaphore()

    def greet(device):
        pl.semaphore_signal(barrier, inc=1, device_id=device, device_id_type=MESH)

    for o in range(1, NY):
        greet(dev(block * NY + yo(o), tp))
    for o in range(1, NZL * NX):
        greet(dev(lax.rem(block + o, NZL * NX) * NY + y, tp))
    greet(dev(section, zh * 2 + 1 - core))

    @pl.when(jnp.logical_not(same))
    def _():
        for o in range(NY):
            greet(dev(plane + yo(o), turned))

    for zz in range(NZL):
        for hh in range(NZH):
            @pl.when(jnp.logical_not(jnp.logical_and(same, jnp.logical_and(zl == zz, zh == hh))))
            def _(zz=zz, hh=hh):
                greet(dev(zz * 32 + x * NY + y, hh * 2 + zl))

    nch = ck.shape[1] // CHUNK

    def chunk_copies(i):
        rows = pl.ds(i * CHUNK, CHUNK)
        return (
            pltpu.make_async_copy(ck.at[0, rows], k.at[rows], ksem.at[i]),
            pltpu.make_async_copy(cv.at[0, rows], v.at[rows, pl.ds(0, HD)], vsem.at[i]),
        )

    for i in range(nch):
        for c in chunk_copies(i):
            c.start()

    for c in small[:3]:
        c.wait()
    for j in range(4):
        piece = dq[j].astype(jnp.float32)
        for h in range(HEADS):
            qf[pl.ds(j * 16 + h, 2, stride=8), :] = piece[:, h * HD:(h + 1) * HD]
        kvf[2 * j:2 * j + 2, :] = dk[j].astype(jnp.float32)
        kvf[8 + 2 * j:10 + 2 * j, :] = dv[j].astype(jnp.float32)
    g1[y, 0:64, :] = qf[...].astype(jnp.bfloat16)
    g1[y, 64:80, :] = kvf[...].astype(jnp.bfloat16)

    pl.semaphore_wait(
        barrier, (NY - 1) + (NZL * NX - 1) + 1 + jnp.where(same, NZL * NZH - 1, NY + NZL * NZH)
    )

    sent = []
    for o in FAR:
        c = remote(g1.at[y], g1.at[y], g1s.at[o], g1r.at[o], dev(block * NY + yo(o), tp))
        c.start()
        sent.append(c)
    w_copy = pltpu.make_async_copy(w_hbm, w, wsem)
    w_swap = remote(w_hbm, w, wss, wsr, dev(plane + y, turned))

    @pl.when(same)
    def _():
        w_copy.start()

    @pl.when(jnp.logical_not(same))
    def _():
        w_swap.start()

    for c in small[3:]:
        c.wait()
    for h in range(HEADS):
        qs[h * SPAN:(h + 1) * SPAN, :] = sq[:, h * HD:(h + 1) * HD]
    svx[:, HD:] = jnp.ones((SPAN, HD), jnp.bfloat16)
    n_rows = HEADS * SPAN
    first = dot(qs[...], sk[...], NT)
    shape = (n_rows, SPAN)
    first = jnp.where(iota(shape, 1) <= (iota(shape, 0) & (SPAN - 1)), first, NEG)
    top = jnp.max(first, axis=1, keepdims=True) * LOG2
    weights = jnp.exp2(first * LOG2 - top)
    acc_s[...] = dot(weights.astype(jnp.bfloat16), svx[...])
    m_s[...] = jnp.broadcast_to(top, m_s.shape)
    length = length_ref[0]

    def prepare(i):
        rows = pl.ds(i * CHUNK, CHUNK)
        for c in chunk_copies(i):
            c.wait()
        seen = jnp.where(iota((CHUNK, HD), 0) + i * CHUNK < length, 1.0, 0.0).astype(jnp.bfloat16)
        k[rows, :] = k[rows, :] * seen + k[0:1, :] * (1 - seen)
        v[rows, 0:HD] = v[rows, 0:HD] * seen
        v[rows, HD:] = seen

    def span_chunk(i):
        rows = pl.ds(i * CHUNK, CHUNK)
        s = dot(qs[...], k[rows, :], NT)
        old = m_s[...]
        new = jnp.maximum(old, jnp.max(s, axis=1, keepdims=True) * LOG2)
        p = jnp.exp2(s * LOG2 - new[:, 0:1])
        shrink = jnp.exp2(old - new)
        m_s[...] = new
        part = dot(p.astype(jnp.bfloat16), v[rows, :])
        acc_s[:, 0:HD] = acc_s[:, 0:HD] * shrink + part[:, 0:HD]
        acc_s[:, HD:] = acc_s[:, HD:] * shrink + part[:, HD:]

    for i in range(3):
        prepare(i)
        span_chunk(i)

    for o in NEAR[1:]:
        slot = yo(-o)
        remote(g1.at[slot], g1.at[slot], g1s.at[o], g1r.at[o], dev(block * NY + yo(o), tp)).wait_recv()

    owner_of = (iota((16, HD), 0) & 7) // 2
    sent2 = []
    for o in (6, 2, 5, 7, 1, 3, 4, 0):
        to = lax.rem(block + o, NZL * NX)
        own = jnp.zeros((16, HD), jnp.float32)
        for j in range(4):
            at = groups[j, to * NY + y] & (NY - 1)
            s2[to, j * 16:(j + 1) * 16, :] = g1[at, j * 16:(j + 1) * 16, :]
            own = jnp.where(owner_of == j, g1[at, 64:80, :].astype(jnp.float32), own)
        s2[to, 64:80, :] = own.astype(jnp.bfloat16)
        if o:
            c = remote(s2.at[to], r2.at[block], g2s.at[o], g2r.at[o], dev(to * NY + y, tp))
            c.start()
            sent2.append(c)
    r2[block] = s2[block]

    for i in range(3, nch):
        prepare(i)
    for i in range(3, 5):
        span_chunk(i)

    for o in range(1, NZL * NX):
        slot = lax.rem(block + NZL * NX - o, NZL * NX)
        remote(s2.at[slot], r2.at[slot], g2s.at[o], g2r.at[o], dev(slot * NY + y, tp)).wait_recv()
    own = jnp.zeros((16, HD), jnp.float32)
    for j in range(4):
        at = lax.shift_right_logical(groups[j, section], 3)
        qf[j * 16:(j + 1) * 16, :] = r2[at, j * 16:(j + 1) * 16, :].astype(jnp.float32)
        own = jnp.where(owner_of == j, r2[at, 64:80, :].astype(jnp.float32), own)

    for h in range(0, HEADS, 2):
        pair = [qf[pl.ds(h + e, 8, stride=8), :] for e in range(2)]
        sel[h * 8:h * 8 + 16, :] = jnp.concatenate(pair, axis=0).astype(jnp.bfloat16)
    query = sel[...]
    own_k = own.astype(jnp.bfloat16)
    own_v = jnp.concatenate([own[8:16], own[0:8]], axis=0).astype(jnp.bfloat16)
    own_v = jnp.concatenate([own_v, jnp.ones((16, HD), jnp.bfloat16)], axis=1)
    s_ctx = dot(query, k[...], NT)
    s_blk = dot(query, sk[...], NT)
    s_own = dot(query, own_k, NT)
    r16, c16 = iota((64, 16), 0), iota((64, 16), 1)
    fits = jnp.logical_and(c16 // 2 == (r16 // 2) % 4, c16 % 2 <= r16 % 2)
    s_own = jnp.where(fits, s_own, NEG)
    top = jnp.maximum(
        jnp.maximum(jnp.max(s_ctx, axis=1, keepdims=True), jnp.max(s_blk, axis=1, keepdims=True)),
        jnp.max(s_own, axis=1, keepdims=True),
    ) * LOG2
    total = dot(jnp.exp2(s_ctx * LOG2 - top).astype(jnp.bfloat16), v[...])
    total += dot(jnp.exp2(s_blk * LOG2 - top).astype(jnp.bfloat16), svx[...])
    total += dot(jnp.exp2(s_own * LOG2 - top).astype(jnp.bfloat16), own_v)
    msg[...] = (total[:, 0:HD] / total[:, HD:]).astype(jnp.bfloat16)

    sent3 = []
    for o in NEAR:
        c = remote(msg, buf.at[section], p1s.at[o], p1r.at[o], dev(plane + yo(o), turned))
        if o:
            c.start()
            sent3.append(c)
        else:
            pl.when(jnp.logical_not(same))(c.start)

            @pl.when(same)
            def _():
                buf[section] = msg[...]

    for i in range(5, nch):
        span_chunk(i)
    for h in range(HEADS):
        rows = slice(h * SPAN, (h + 1) * SPAN)
        span_ref[0, :, h * HD:(h + 1) * HD] = (acc_s[rows, 0:HD] / acc_s[rows, HD:]).astype(jnp.bfloat16)

    lane = iota((16, 512), 1)
    sub = iota((16, 512), 0)
    col = (sub & 7) // 2

    def one_hot(i, _):
        want = jnp.zeros((16, 512), jnp.int32)
        for half in range(2):
            for j in range(4):
                want = jnp.where(
                    jnp.logical_and(sub // 8 == half, col == j), groups[j, 2 * i + half], want
                )
        hit = ((want * 8 + (sub & 7) + (NZH - zh) * 128) & 511) == lane
        pt[pl.ds(pl.multiple_of(i * 16, 16), 16), :] = jnp.where(hit, 1.0, 0.0).astype(jnp.bfloat16)
        return 0

    lax.fori_loop(0, 32, one_hot, 0)

    def sibling(half, o):
        part = buf4.at[half, :, yo(-o)]
        return remote(part, part, cs.at[o], cr.at[o], dev(section, zh * 2 + 1 - core))

    for o in NEAR:
        slot = plane + yo(-o)
        c = remote(msg, buf.at[slot], p1s.at[o], p1r.at[o], dev(plane + yo(o), turned))
        if o:
            c.wait_recv()
        else:
            pl.when(jnp.logical_not(same))(c.wait_recv)
        for d in (2, 1, 3):
            c = remote(
                buf.at[slot], buf.at[slot], p2s.at[o, d], p2r.at[o, d],
                dev(zl * 32 + xo(d) * NY + y, tp),
            )
            c.start()
            sent3.append(c)
    for o in NEAR:
        for d in NEAR_X:
            slot = core * 32 + xo(-d) * NY + yo(-o)
            remote(
                buf.at[slot], buf.at[slot], p2s.at[o, d], p2r.at[o, d],
                dev(zl * 32 + xo(d) * NY + y, tp),
            ).wait_recv()
        c = sibling(core, o)
        c.start()
        sent3.append(c)
    pl.when(same)(w_copy.wait)
    pl.when(jnp.logical_not(same))(w_swap.wait_recv)

    def project(half):
        full = None
        for pair in range(HEADS // 2):
            at = pair * 2 * HD
            both = jnp.concatenate([w[at:at + HD, :], w[at + HD:at + 2 * HD, :]], axis=1)
            x_pair = buf[pl.ds(half * 32, 32), pair * 16:(pair + 1) * 16, :].reshape(512, HD)
            part = dot(x_pair, both)
            full = part if full is None else full + part
        full = full.reshape(32, 16, 2 * HD)
        rows = (full[:, 0:8, 0:HD] + full[:, 8:16, HD:]).reshape(256, HD)
        zp[pl.ds(pl.multiple_of(half * 256, 256), 256), :] = rows.astype(jnp.bfloat16)

    project(core)
    for o in NEAR:
        sibling(1 - core, o).wait_recv()
    project(1 - core)

    sent4 = []
    for hh in (2, 1, 3, 0):
        rows = dot(pt[:, hh * 128:(hh + 1) * 128], zp[...], TN)
        zs[hh * 128:(hh + 1) * 128, :] = rows.astype(jnp.bfloat16)
        for e in range(2):
            at = pl.ds(hh * 128 + e * 64, 64)
            to = lax.rem(zh + hh, NZH) * 2 + e
            c = remote(zs.at[at], rr.at[turned], rs.at[hh * 2 + e], rrs.at[turned], dev(plane + y, to))
            if hh:
                c.start()
                sent4.append(c.wait_send)
                continue
            mine = jnp.logical_and(same, core == e)
            other = jnp.logical_not(mine)
            pl.when(other)(c.start)
            sent4.append(functools.partial(pl.when(other), c.wait_send))

            @pl.when(mine)
            def _():
                rr[turned] = zs[at, :]

    out = None
    for s in range(8):
        c = remote(zs.at[pl.ds(s * 64, 64)], rr.at[s], rs.at[s], rrs.at[s], dev(plane + y, s))
        pl.when(jnp.logical_not(jnp.logical_and(same, turned == s)))(c.wait_recv)
    for s in range(8):
        part = rr[s].astype(jnp.float32)
        out = part if out is None else out + part
    proj_ref[...] = out.astype(jnp.bfloat16)

    for c in sent + sent2 + sent3:
        c.wait_send()
    pl.when(jnp.logical_not(same))(w_swap.wait_send)
    c = remote(msg, buf.at[section], p1s.at[0], p1r.at[0], dev(plane + y, turned))
    pl.when(jnp.logical_not(same))(c.wait_send)
    for wait in sent4:
        wait()


def body(ctx_keys, ctx_values, span_q, span_k, span_v, lengths, group_lists, dec_q, dec_k, dec_v, out_weight):
    ctx = ctx_keys.shape[1]
    bf, f32 = jnp.bfloat16, jnp.float32
    vmem = pl.BlockSpec(memory_space=pltpu.VMEM)
    hbm = pl.BlockSpec(memory_space=pl.ANY)
    dma = pltpu.SemaphoreType.DMA
    span_out, proj = pl.pallas_call(
        kernel,
        name="block_and_decode_attention",
        out_shape=(
            pltpu.VMEM(span_q.shape, bf),
            pltpu.VMEM((64, HD), bf),
        ),
        in_specs=[pl.BlockSpec(memory_space=pltpu.SMEM)] + [hbm] * 10,
        out_specs=(vmem, vmem),
        scratch_shapes=[
            pltpu.VMEM((SPAN, HEADS * HD), bf),
            pltpu.VMEM((SPAN, HD), bf),
            pltpu.VMEM((SPAN, 2 * HD), bf),
            pltpu.SMEM((4, 64), jnp.int32),
            pltpu.VMEM(dec_q.shape, bf),
            pltpu.VMEM(dec_k.shape, bf),
            pltpu.VMEM(dec_v.shape, bf),
            dma((8,)),
            pltpu.VMEM((ctx, HD), bf),
            pltpu.VMEM((ctx, 2 * HD), bf),
            pltpu.VMEM((HEADS * SPAN, HD), bf),
            pltpu.VMEM((HEADS * SPAN, HD), f32),
            pltpu.VMEM((HEADS * SPAN, 2 * HD), f32),
            pltpu.VMEM((64, HD), f32),
            pltpu.VMEM((16, HD), f32),
            pltpu.VMEM((8, 80, HD), bf),
            pltpu.VMEM((8, 80, HD), bf),
            pltpu.VMEM((8, 80, HD), bf),
            pltpu.VMEM((64, HD), bf),
            pltpu.VMEM((64, HD), bf),
            pltpu.VMEM((64, 64, HD), bf),
            pltpu.VMEM((HEADS * HD, HD), bf),
            pltpu.VMEM((512, 512), bf),
            pltpu.VMEM((512, HD), bf),
            pltpu.VMEM((512, HD), bf),
            pltpu.VMEM((8, 64, HD), bf),
            dma((ctx // CHUNK,)), dma((ctx // CHUNK,)), dma,
            dma((8,)), dma((8,)), dma((8,)), dma((8,)), dma, dma,
            dma((8,)), dma((8,)), dma((8, 4)), dma((8, 4)), dma((8,)), dma((8,)),
            dma((8,)), dma((8,)),
        ],
        compiler_params=pltpu.CompilerParams(
            collective_id=0, has_side_effects=True, vmem_limit_bytes=58 << 20
        ),
        cost_estimate=pl.CostEstimate(flops=2_000_000_000, bytes_accessed=4 << 20, transcendentals=3_600_000),
    )(
        lengths,
        *(
            pltpu.with_memory_space_constraint(a, pltpu.HBM)
            for a in (
                ctx_keys, ctx_values, span_q, span_k, span_v, group_lists.T, dec_q, dec_k, dec_v, out_weight
            )
        ),
    )
    return span_out, proj.reshape(32, 2, HD)


def solution(mesh):
    in_specs = (
        P("section", None, "tp"),
        P("section", None, "tp"),
        P("section", None, "tp"),
        P("section", None, "tp"),
        P("section", None, "tp"),
        P("section"),
        P(),
        P("section", None, "tp"),
        P("section", None, "tp"),
        P("section", None, "tp"),
        P("tp", "section"),
    )
    out_specs = (P("section", None, "tp"), P("tp", None, "section"))
    return jax.shard_map(body, mesh=mesh, in_specs=in_specs, out_specs=out_specs, check_vma=False)
```

```python
import functools
import math

import jax
import jax.numpy as jnp
from jax import lax
from jax.experimental import pallas as pl
from jax.experimental.pallas import tpu as pltpu
from jax.sharding import PartitionSpec as P

HD = 128
NX, NY, NZL, NZH = 4, 8, 2, 4
HEADS = 8
SPAN = 64
CHUNK = 1024
LOG2 = HD**-0.5 * math.log2(math.e)
NEG = -1e30
MESH = pl.DeviceIdType.MESH
NT = (((1,), (1,)), ((), ()))
TN = (((0,), (0,)), ((), ()))
NN = (((1,), (0,)), ((), ()))
NEAR = (0, 1, 7, 2, 6, 3, 5, 4)
NEAR_X = (1, 3, 2)
FAR = (4, 3, 5, 2, 6, 1, 7)


def dot(a, b, dims=NN):
    return lax.dot_general(a, b, dims, preferred_element_type=jnp.float32)


def iota(shape, dim):
    return lax.broadcasted_iota(jnp.int32, shape, dim)


def kernel(
    length_ref, ck, cv, sq_hbm, sk_hbm, sv_hbm, groups_hbm, dq_hbm, dk_hbm, dv_hbm, w_hbm,
    span_ref, proj_ref,
    sq, sk, svx, groups, dq, dk, dv, insem,
    k, v, qs, m_s, acc_s, qf, kvf, g1, s2, r2, sel, msg, buf, w, pt, zp, zs, rr,
    ksem, vsem, wsem, g1s, g1r, g2s, g2r, wss, wsr, p1s, p1r, p2s, p2r, cs, cr, rs, rrs,
):
    section, tp = lax.axis_index("section"), lax.axis_index("tp")
    zl, x, y = section // 32, lax.rem(section // NY, NX), lax.rem(section, NY)
    zh, core = tp // 2, lax.rem(tp, 2)
    block = section // NY

    def dev(sec, t):
        return {"section": sec, "tp": t}

    def remote(src, dst, ssem, rsem, device):
        return pltpu.make_async_remote_copy(
            src_ref=src, dst_ref=dst, send_sem=ssem, recv_sem=rsem, device_id=device, device_id_type=MESH
        )

    def yo(o):
        return lax.rem(y + o + NY, NY)

    def xo(o):
        return lax.rem(x + o + NX, NX)

    same = zl == core
    buf4 = buf.reshape(NZL, NX, NY, 64, HD)
    plane = core * 32 + x * NY
    turned = zh * 2 + zl

    small = []
    for i, (src, dst) in enumerate((
        (dq_hbm, dq), (dk_hbm, dk), (dv_hbm, dv), (sq_hbm.at[0], sq), (sk_hbm.at[0], sk),
        (sv_hbm.at[0], svx.at[:, pl.ds(0, HD)]), (groups_hbm, groups),
    )):
        c = pltpu.make_async_copy(src, dst, insem.at[i])
        c.start()
        small.append(c)

    barrier = pltpu.get_barrier_semaphore()

    def greet(device):
        pl.semaphore_signal(barrier, inc=1, device_id=device, device_id_type=MESH)

    for o in range(1, NY):
        greet(dev(block * NY + yo(o), tp))
    for o in range(1, NZL * NX):
        greet(dev(lax.rem(block + o, NZL * NX) * NY + y, tp))
    greet(dev(section, zh * 2 + 1 - core))

    @pl.when(jnp.logical_not(same))
    def _():
        for o in range(NY):
            greet(dev(plane + yo(o), turned))

    for zz in range(NZL):
        for hh in range(NZH):
            @pl.when(jnp.logical_not(jnp.logical_and(same, jnp.logical_and(zl == zz, zh == hh))))
            def _(zz=zz, hh=hh):
                greet(dev(zz * 32 + x * NY + y, hh * 2 + zl))

    nch = ck.shape[1] // CHUNK

    def chunk_copies(i):
        rows = pl.ds(i * CHUNK, CHUNK)
        return (
            pltpu.make_async_copy(ck.at[0, rows], k.at[rows], ksem.at[i]),
            pltpu.make_async_copy(cv.at[0, rows], v.at[rows, pl.ds(0, HD)], vsem.at[i]),
        )

    for i in range(nch):
        for c in chunk_copies(i):
            c.start()

    for c in small[:3]:
        c.wait()
    for j in range(4):
        piece = dq[j].astype(jnp.float32)
        for h in range(HEADS):
            qf[pl.ds(j * 16 + h, 2, stride=8), :] = piece[:, h * HD:(h + 1) * HD]
        kvf[2 * j:2 * j + 2, :] = dk[j].astype(jnp.float32)
        kvf[8 + 2 * j:10 + 2 * j, :] = dv[j].astype(jnp.float32)
    g1[y, 0:64, :] = qf[...].astype(jnp.bfloat16)
    g1[y, 64:80, :] = kvf[...].astype(jnp.bfloat16)

    pl.semaphore_wait(
        barrier, (NY - 1) + (NZL * NX - 1) + 1 + jnp.where(same, NZL * NZH - 1, NY + NZL * NZH)
    )

    sent = []
    for o in FAR:
        c = remote(g1.at[y], g1.at[y], g1s.at[o], g1r.at[o], dev(block * NY + yo(o), tp))
        c.start()
        sent.append(c)
    w_copy = pltpu.make_async_copy(w_hbm, w, wsem)
    w_swap = remote(w_hbm, w, wss, wsr, dev(plane + y, turned))

    @pl.when(same)
    def _():
        w_copy.start()

    @pl.when(jnp.logical_not(same))
    def _():
        w_swap.start()

    for c in small[3:]:
        c.wait()
    for h in range(HEADS):
        qs[h * SPAN:(h + 1) * SPAN, :] = sq[:, h * HD:(h + 1) * HD]
    svx[:, HD:] = jnp.ones((SPAN, HD), jnp.bfloat16)
    n_rows = HEADS * SPAN
    first = dot(qs[...], sk[...], NT)
    shape = (n_rows, SPAN)
    first = jnp.where(iota(shape, 1) <= (iota(shape, 0) & (SPAN - 1)), first, NEG)
    top = jnp.max(first, axis=1, keepdims=True) * LOG2
    weights = jnp.exp2(first * LOG2 - top)
    acc_s[...] = dot(weights.astype(jnp.bfloat16), svx[...])
    m_s[...] = jnp.broadcast_to(top, m_s.shape)
    length = length_ref[0]

    def prepare(i):
        rows = pl.ds(i * CHUNK, CHUNK)
        for c in chunk_copies(i):
            c.wait()
        seen = jnp.where(iota((CHUNK, HD), 0) + i * CHUNK < length, 1.0, 0.0).astype(jnp.bfloat16)
        k[rows, :] = k[rows, :] * seen + k[0:1, :] * (1 - seen)
        v[rows, 0:HD] = v[rows, 0:HD] * seen
        v[rows, HD:] = seen

    def span_chunk(i):
        rows = pl.ds(i * CHUNK, CHUNK)
        s = dot(qs[...], k[rows, :], NT)
        old = m_s[...]
        new = jnp.maximum(old, jnp.max(s, axis=1, keepdims=True) * LOG2)
        p = jnp.exp2(s * LOG2 - new[:, 0:1])
        shrink = jnp.exp2(old - new)
        m_s[...] = new
        part = dot(p.astype(jnp.bfloat16), v[rows, :])
        acc_s[:, 0:HD] = acc_s[:, 0:HD] * shrink + part[:, 0:HD]
        acc_s[:, HD:] = acc_s[:, HD:] * shrink + part[:, HD:]

    for i in range(2):
        prepare(i)
        span_chunk(i)

    for o in NEAR[1:]:
        slot = yo(-o)
        remote(g1.at[slot], g1.at[slot], g1s.at[o], g1r.at[o], dev(block * NY + yo(o), tp)).wait_recv()

    owner_of = (iota((16, HD), 0) & 7) // 2
    sent2 = []
    for o in (6, 2, 5, 7, 1, 3, 4, 0):
        to = lax.rem(block + o, NZL * NX)
        own = jnp.zeros((16, HD), jnp.float32)
        for j in range(4):
            at = groups[j, to * NY + y] & (NY - 1)
            s2[to, j * 16:(j + 1) * 16, :] = g1[at, j * 16:(j + 1) * 16, :]
            own = jnp.where(owner_of == j, g1[at, 64:80, :].astype(jnp.float32), own)
        s2[to, 64:80, :] = own.astype(jnp.bfloat16)
        if o:
            c = remote(s2.at[to], r2.at[block], g2s.at[o], g2r.at[o], dev(to * NY + y, tp))
            c.start()
            sent2.append(c)
    r2[block] = s2[block]

    for i in range(2, nch):
        prepare(i)
    for i in range(2, 5):
        span_chunk(i)

    for o in range(1, NZL * NX):
        slot = lax.rem(block + NZL * NX - o, NZL * NX)
        remote(s2.at[slot], r2.at[slot], g2s.at[o], g2r.at[o], dev(slot * NY + y, tp)).wait_recv()
    own = jnp.zeros((16, HD), jnp.float32)
    for j in range(4):
        at = lax.shift_right_logical(groups[j, section], 3)
        qf[j * 16:(j + 1) * 16, :] = r2[at, j * 16:(j + 1) * 16, :].astype(jnp.float32)
        own = jnp.where(owner_of == j, r2[at, 64:80, :].astype(jnp.float32), own)

    for h in range(0, HEADS, 2):
        pair = [qf[pl.ds(h + e, 8, stride=8), :] for e in range(2)]
        sel[h * 8:h * 8 + 16, :] = jnp.concatenate(pair, axis=0).astype(jnp.bfloat16)
    query = sel[...]
    own_k = own.astype(jnp.bfloat16)
    own_v = jnp.concatenate([own[8:16], own[0:8]], axis=0).astype(jnp.bfloat16)
    own_v = jnp.concatenate([own_v, jnp.ones((16, HD), jnp.bfloat16)], axis=1)
    s_ctx = dot(query, k[...], NT)
    s_blk = dot(query, sk[...], NT)
    s_own = dot(query, own_k, NT)
    r16, c16 = iota((64, 16), 0), iota((64, 16), 1)
    fits = jnp.logical_and(c16 // 2 == (r16 // 2) % 4, c16 % 2 <= r16 % 2)
    s_own = jnp.where(fits, s_own, NEG)
    top = jnp.maximum(
        jnp.maximum(jnp.max(s_ctx, axis=1, keepdims=True), jnp.max(s_blk, axis=1, keepdims=True)),
        jnp.max(s_own, axis=1, keepdims=True),
    ) * LOG2
    total = dot(jnp.exp2(s_ctx * LOG2 - top).astype(jnp.bfloat16), v[...])
    total += dot(jnp.exp2(s_blk * LOG2 - top).astype(jnp.bfloat16), svx[...])
    total += dot(jnp.exp2(s_own * LOG2 - top).astype(jnp.bfloat16), own_v)
    msg[...] = (total[:, 0:HD] / total[:, HD:]).astype(jnp.bfloat16)

    sent3 = []
    for o in NEAR:
        c = remote(msg, buf.at[section], p1s.at[o], p1r.at[o], dev(plane + yo(o), turned))
        if o:
            c.start()
            sent3.append(c)
        else:
            pl.when(jnp.logical_not(same))(c.start)

            @pl.when(same)
            def _():
                buf[section] = msg[...]

    for i in range(5, nch):
        span_chunk(i)
    for h in range(HEADS):
        rows = slice(h * SPAN, (h + 1) * SPAN)
        span_ref[0, :, h * HD:(h + 1) * HD] = (acc_s[rows, 0:HD] / acc_s[rows, HD:]).astype(jnp.bfloat16)

    lane = iota((16, 512), 1)
    sub = iota((16, 512), 0)
    col = (sub & 7) // 2

    def one_hot(i, _):
        want = jnp.zeros((16, 512), jnp.int32)
        for half in range(2):
            for j in range(4):
                want = jnp.where(
                    jnp.logical_and(sub // 8 == half, col == j), groups[j, 2 * i + half], want
                )
        hit = ((want * 8 + (sub & 7) + (NZH - zh) * 128) & 511) == lane
        pt[pl.ds(pl.multiple_of(i * 16, 16), 16), :] = jnp.where(hit, 1.0, 0.0).astype(jnp.bfloat16)
        return 0

    lax.fori_loop(0, 32, one_hot, 0)

    def sibling(half, o):
        part = buf4.at[half, :, yo(-o)]
        return remote(part, part, cs.at[o], cr.at[o], dev(section, zh * 2 + 1 - core))

    for o in NEAR:
        slot = plane + yo(-o)
        c = remote(msg, buf.at[slot], p1s.at[o], p1r.at[o], dev(plane + yo(o), turned))
        if o:
            c.wait_recv()
        else:
            pl.when(jnp.logical_not(same))(c.wait_recv)
        for d in (2, 1, 3):
            c = remote(
                buf.at[slot], buf.at[slot], p2s.at[o, d], p2r.at[o, d],
                dev(zl * 32 + xo(d) * NY + y, tp),
            )
            c.start()
            sent3.append(c)
    for o in NEAR:
        for d in NEAR_X:
            slot = core * 32 + xo(-d) * NY + yo(-o)
            remote(
                buf.at[slot], buf.at[slot], p2s.at[o, d], p2r.at[o, d],
                dev(zl * 32 + xo(d) * NY + y, tp),
            ).wait_recv()
        c = sibling(core, o)
        c.start()
        sent3.append(c)
    pl.when(same)(w_copy.wait)
    pl.when(jnp.logical_not(same))(w_swap.wait_recv)

    def project(half):
        full = None
        for pair in range(HEADS // 2):
            at = pair * 2 * HD
            both = jnp.concatenate([w[at:at + HD, :], w[at + HD:at + 2 * HD, :]], axis=1)
            x_pair = buf[pl.ds(half * 32, 32), pair * 16:(pair + 1) * 16, :].reshape(512, HD)
            part = dot(x_pair, both)
            full = part if full is None else full + part
        full = full.reshape(32, 16, 2 * HD)
        rows = (full[:, 0:8, 0:HD] + full[:, 8:16, HD:]).reshape(256, HD)
        zp[pl.ds(pl.multiple_of(half * 256, 256), 256), :] = rows.astype(jnp.bfloat16)

    project(core)
    for o in NEAR:
        sibling(1 - core, o).wait_recv()
    project(1 - core)

    sent4 = []
    for hh in (2, 1, 3, 0):
        rows = dot(pt[:, hh * 128:(hh + 1) * 128], zp[...], TN)
        zs[hh * 128:(hh + 1) * 128, :] = rows.astype(jnp.bfloat16)
        for e in range(2):
            at = pl.ds(hh * 128 + e * 64, 64)
            to = lax.rem(zh + hh, NZH) * 2 + e
            c = remote(zs.at[at], rr.at[turned], rs.at[hh * 2 + e], rrs.at[turned], dev(plane + y, to))
            if hh:
                c.start()
                sent4.append(c.wait_send)
                continue
            mine = jnp.logical_and(same, core == e)
            other = jnp.logical_not(mine)
            pl.when(other)(c.start)
            sent4.append(functools.partial(pl.when(other), c.wait_send))

            @pl.when(mine)
            def _():
                rr[turned] = zs[at, :]

    out = None
    for s in range(8):
        c = remote(zs.at[pl.ds(s * 64, 64)], rr.at[s], rs.at[s], rrs.at[s], dev(plane + y, s))
        pl.when(jnp.logical_not(jnp.logical_and(same, turned == s)))(c.wait_recv)
        part = rr[s].astype(jnp.float32)
        out = part if out is None else out + part
    proj_ref[...] = out.astype(jnp.bfloat16)

    for c in sent + sent2 + sent3:
        c.wait_send()
    pl.when(jnp.logical_not(same))(w_swap.wait_send)
    c = remote(msg, buf.at[section], p1s.at[0], p1r.at[0], dev(plane + y, turned))
    pl.when(jnp.logical_not(same))(c.wait_send)
    for wait in sent4:
        wait()


def body(ctx_keys, ctx_values, span_q, span_k, span_v, lengths, group_lists, dec_q, dec_k, dec_v, out_weight):
    ctx = ctx_keys.shape[1]
    bf, f32 = jnp.bfloat16, jnp.float32
    vmem = pl.BlockSpec(memory_space=pltpu.VMEM)
    hbm = pl.BlockSpec(memory_space=pl.ANY)
    dma = pltpu.SemaphoreType.DMA
    span_out, proj = pl.pallas_call(
        kernel,
        name="block_and_decode_attention",
        out_shape=(
            pltpu.VMEM(span_q.shape, bf),
            pltpu.VMEM((64, HD), bf),
        ),
        in_specs=[pl.BlockSpec(memory_space=pltpu.SMEM)] + [hbm] * 10,
        out_specs=(vmem, vmem),
        scratch_shapes=[
            pltpu.VMEM((SPAN, HEADS * HD), bf),
            pltpu.VMEM((SPAN, HD), bf),
            pltpu.VMEM((SPAN, 2 * HD), bf),
            pltpu.SMEM((4, 64), jnp.int32),
            pltpu.VMEM(dec_q.shape, bf),
            pltpu.VMEM(dec_k.shape, bf),
            pltpu.VMEM(dec_v.shape, bf),
            dma((8,)),
            pltpu.VMEM((ctx, HD), bf),
            pltpu.VMEM((ctx, 2 * HD), bf),
            pltpu.VMEM((HEADS * SPAN, HD), bf),
            pltpu.VMEM((HEADS * SPAN, HD), f32),
            pltpu.VMEM((HEADS * SPAN, 2 * HD), f32),
            pltpu.VMEM((64, HD), f32),
            pltpu.VMEM((16, HD), f32),
            pltpu.VMEM((8, 80, HD), bf),
            pltpu.VMEM((8, 80, HD), bf),
            pltpu.VMEM((8, 80, HD), bf),
            pltpu.VMEM((64, HD), bf),
            pltpu.VMEM((64, HD), bf),
            pltpu.VMEM((64, 64, HD), bf),
            pltpu.VMEM((HEADS * HD, HD), bf),
            pltpu.VMEM((512, 512), bf),
            pltpu.VMEM((512, HD), bf),
            pltpu.VMEM((512, HD), bf),
            pltpu.VMEM((8, 64, HD), bf),
            dma((ctx // CHUNK,)), dma((ctx // CHUNK,)), dma,
            dma((8,)), dma((8,)), dma((8,)), dma((8,)), dma, dma,
            dma((8,)), dma((8,)), dma((8, 4)), dma((8, 4)), dma((8,)), dma((8,)),
            dma((8,)), dma((8,)),
        ],
        compiler_params=pltpu.CompilerParams(
            collective_id=0, has_side_effects=True, vmem_limit_bytes=58 << 20
        ),
        cost_estimate=pl.CostEstimate(flops=2_000_000_000, bytes_accessed=4 << 20, transcendentals=3_600_000),
    )(
        lengths,
        *(
            pltpu.with_memory_space_constraint(a, pltpu.HBM)
            for a in (
                ctx_keys, ctx_values, span_q, span_k, span_v, group_lists.T, dec_q, dec_k, dec_v, out_weight
            )
        ),
    )
    return span_out, proj.reshape(32, 2, HD)


def solution(mesh):
    in_specs = (
        P("section", None, "tp"),
        P("section", None, "tp"),
        P("section", None, "tp"),
        P("section", None, "tp"),
        P("section", None, "tp"),
        P("section"),
        P(),
        P("section", None, "tp"),
        P("section", None, "tp"),
        P("section", None, "tp"),
        P("tp", "section"),
    )
    out_specs = (P("section", None, "tp"), P("tp", None, "section"))
    return jax.shard_map(body, mesh=mesh, in_specs=in_specs, out_specs=out_specs, check_vma=False)
```
